32 devices in a mesh: groups: 2 (over y), seq: 4 (over z), tile: 2 (over x), chan: 2 (over core).
Axes of the slice: x: 2, y: 2, z: 4, core: 2. Of those that a mesh axis runs over, the one named last changes fastest.
Arguments:
- latents: bfloat16 [2, 7680, 384], P('tile', ('groups', 'seq'), 'chan'), parts along dimension 1, may hold values from -6 to 6
- norm_gain: float32 [384], replicated, may hold values from 0.1 to 1.9
- conv_weight: bfloat16 [3, 3, 3, 384, 384], P(None, None, None, None, 'chan'), may hold values from -0.0625 to 0.0625
- conv_bias: float32 [384], P('chan'), may hold values from -3 to 3
- upsample_weight: bfloat16 [3, 3, 384, 192], P(None, None, None, 'chan'), may hold values from -0.109375 to 0.109375
- upsample_bias: float32 [192], P('chan'), may hold values from -3 to 3
Outputs:
- decoded: bfloat16 [8, 192, 20, 384], P(None, ('groups', 'tile'), 'seq', 'chan'), parts along dimension 1
The draws below stay inside these ranges and needn't reach their ends.
There are 2 independent parts, one for each index of `groups`. The reference program is written for one: setup_inputs(seed, part) draws one part's arguments, and reference() takes and returns one part's arrays. A program takes and returns all parts, laid end to end along the dimension named above; an argument that names none is the same for every part. Nothing has to cross between parts.
All inputs are finite; a program needn't handle non-finite values.
Results may differ from the reference program's by a relative error of at most 0.005.
Values may be sent and summed in bfloat16 or wider, within the bound.
A program may use at most 64 MiB of HBM per device.

```python
import jax
import jax.numpy as jnp
from jax import lax

C = 384
CO = 192
FRAMES = 8
ROWS_DEV = 24
BLOCKS = 2
H = 48
W = 20
TOKQ = 3840


def block_levels(own_key, shape, pieces, low, largest):
    gain, own = 1.0, jax.random.fold_in(own_key, 6)
    for dim, parts in pieces:
        draws = jnp.exp(jax.random.uniform(jax.random.fold_in(own, dim), (parts,), jnp.float32, low / len(pieces), largest / len(pieces)))
        gain = gain * jnp.repeat(draws, shape[dim] // parts).reshape([-1 if axis == dim else 1 for axis in range(len(shape))])
    return gain


def centred(own_key, dims, scale, reach, cuts=(), held_as=jnp.bfloat16):
    entries = scale * jax.random.normal(own_key, dims, jnp.float32)
    if cuts:
        entries = entries * block_levels(own_key, dims, cuts, -0.22, 0.18)
    return jnp.clip(entries, -reach, reach).astype(held_as)


def setup_inputs(seed: int = 0, part: int = 0) -> dict:
    streams_of = jax.random.split(jax.random.key(seed), 7)
    own_keys = jax.random.split(jax.random.fold_in(streams_of[6], part), 7)
    latents = centred(own_keys[0], (BLOCKS, TOKQ, C), 1.0, 6.0, ((0, 2), (1, 4), (2, 2)))
    norm_gain = jnp.clip(1.0 + 0.18 * jax.random.normal(streams_of[1], (C,), jnp.float32), 0.1, 1.9)
    conv_weight = centred(streams_of[2], (3, 3, 3, C, C), (27 * C) ** -0.5, 0.0625, ((4, 2),))
    conv_bias = centred(streams_of[3], (C,), 0.5, 3.0, ((0, 2),), jnp.float32)
    upsample_weight = centred(streams_of[4], (3, 3, C, CO), (9 * C) ** -0.5, 0.109375, ((3, 2),))
    upsample_bias = centred(streams_of[5], (CO,), 0.5, 3.0, ((0, 2),), jnp.float32)
    return dict(latents=latents, norm_gain=norm_gain, conv_weight=conv_weight, conv_bias=conv_bias, upsample_weight=upsample_weight, upsample_bias=upsample_bias)


def reference(latents, norm_gain, conv_weight, conv_bias, upsample_weight, upsample_bias):
    field = latents.reshape(BLOCKS, FRAMES, ROWS_DEV, W, C)
    field = jnp.transpose(field, (1, 0, 2, 3, 4)).reshape(FRAMES, H, W, C)
    values = field.astype(jnp.float32)
    scale = lax.rsqrt(lax.optimization_barrier(jnp.mean(values * values, axis=-1, keepdims=True)) + 1e-06)
    act = jax.nn.silu(values * scale * norm_gain).astype(jnp.bfloat16)
    padded = jnp.pad(act, ((2, 0), (1, 1), (1, 1), (0, 0)))
    conv = lax.conv_general_dilated(padded[None], conv_weight, (1, 1, 1), 'VALID', dimension_numbers=('NDHWC', 'DHWIO', 'NDHWC'), preferred_element_type=jnp.float32)[0]
    middle = (field.astype(jnp.float32) + conv + conv_bias).astype(jnp.bfloat16)
    upsampled = jnp.repeat(jnp.repeat(middle, 2, axis=1), 2, axis=2)
    upsampled = jnp.pad(upsampled, ((0, 0), (1, 1), (1, 1), (0, 0)))
    image = lax.conv_general_dilated(upsampled, upsample_weight, (1, 1), 'VALID', dimension_numbers=('NHWC', 'HWIO', 'NHWC'), preferred_element_type=jnp.float32)
    image = image + upsample_bias
    image = image.reshape(FRAMES, 2 * H, W, 2, CO)
    image = jnp.transpose(image, (0, 1, 2, 4, 3)).reshape(FRAMES, 2 * H, W, 2 * CO)
    return image.astype(jnp.bfloat16)
```

```python
import functools

import jax
import jax.numpy as jnp
from jax import lax
from jax.experimental import pallas as pl
from jax.experimental.pallas import tpu as pltpu
from jax.sharding import PartitionSpec as P

FRAMES = 8
ROWS_DEV = 24
COLS_DEV = 5
PITCH = 32
MESH = pl.DeviceIdType.MESH


norm_eps = 1e-06


def extended(cells, sides, width):
    for axis, dim in sides:
        count = lax.axis_size(axis)
        ends = count - 1
        head = lax.slice_in_dim(cells, 0, width, axis=dim)
        tail = lax.slice_in_dim(cells, cells.shape[dim] - width, cells.shape[dim], axis=dim)
        cells = jnp.concatenate(
            [
                lax.ppermute(tail, axis, [(i, (i + 1) % count) for i in range(ends)]),
                cells,
                lax.ppermute(head, axis, [((i + 1) % count, i) for i in range(ends)]),
            ],
            axis=dim,
        )
    return cells


def activate(padded, norm_gain):
    values = padded.astype(jnp.float32)
    scale = lax.rsqrt(jnp.mean(values * values, axis=-1, keepdims=True) + norm_eps)
    return jax.nn.silu(values * scale * norm_gain).astype(jnp.bfloat16)


def plain_body(latents, norm_gain, conv_weight, conv_bias, upsample_weight, upsample_bias):
    seq_count = lax.axis_size("seq")
    local_chan = conv_bias.shape[0]
    rows_src = FRAMES * ROWS_DEV // seq_count
    whole = lax.all_gather(latents[0], "chan", axis=1, tiled=True)
    arranged = whole.reshape(rows_src, seq_count, COLS_DEV, whole.shape[1])
    regrouped = lax.all_to_all(arranged, "seq", split_axis=1, concat_axis=0, tiled=True)
    full_field = regrouped.reshape(FRAMES, ROWS_DEV, COLS_DEV, whole.shape[1])
    padded = extended(full_field, (("seq", 2), ("tile", 1)), 1)
    field_own = lax.dynamic_slice_in_dim(
        full_field, lax.axis_index("chan") * local_chan, local_chan, 3
    )
    activation = activate(padded, norm_gain)
    shifted = jnp.pad(activation, ((2, 0), (0, 0), (0, 0), (0, 0)))
    conv_out = lax.conv_general_dilated(
        shifted[None],
        conv_weight,
        (1, 1, 1),
        "VALID",
        dimension_numbers=("NDHWC", "DHWIO", "NDHWC"),
        preferred_element_type=jnp.float32,
    )[0]
    middle = (field_own.astype(jnp.float32) + conv_out + conv_bias).astype(jnp.bfloat16)
    middle_rim = extended(middle, (("seq", 2), ("tile", 1)), 1)
    middle_full = lax.all_gather(middle_rim, "chan", axis=3, tiled=True)
    upsampled = jnp.repeat(jnp.repeat(middle_full, 2, axis=1), 2, axis=2)[:, 1:-1, 1:-1, :]
    image = lax.conv_general_dilated(
        upsampled,
        upsample_weight,
        (1, 1),
        "VALID",
        dimension_numbers=("NHWC", "HWIO", "NHWC"),
        preferred_element_type=jnp.float32,
    )
    image = image + upsample_bias
    out_chan = upsample_bias.shape[0]
    image = image.reshape(FRAMES, 2 * ROWS_DEV, COLS_DEV, 2, out_chan)
    image = jnp.transpose(image, (0, 1, 2, 4, 3)).reshape(
        FRAMES, 2 * ROWS_DEV, COLS_DEV, 2 * out_chan
    )
    return image.astype(jnp.bfloat16)


def kernel(S, T, main_ref, tops_ref, bots_ref, gain_ref, cw_ref, cb_ref, uw_ref, ub_ref, out_ref,
           recv, halo, act3, res, wv, wf, mid, up,
           w_sem, a_send, a_recv, f_send, f_recv, h_send, h_recv, g_send, g_recv, m_send, m_recv, e_send, e_recv):
    s, t, c = lax.axis_index("seq"), lax.axis_index("tile"), lax.axis_index("chan")
    other = 1 - c
    wide = COLS_DEV + 2
    nf = FRAMES // S
    half = main_ref.shape[2]
    full = 2 * half

    def weight_copy(dt, dh, dw):
        return pltpu.make_async_copy(
            cw_ref.at[dt, dh, dw],
            wv.at[dt * 3 + dw, pl.ds(dh * full, full)],
            w_sem.at[dt, dh, dw],
        )

    taps = [(dt, dh, dw) for dt in range(3) for dh in range(3) for dw in range(3)]
    for tap in taps:
        weight_copy(*tap).start()

    barrier = pltpu.get_barrier_semaphore()
    size = S * T * 2
    me = (s * T + t) * 2 + c
    for k in range(1, size):
        peer = (me + k) % size
        pl.semaphore_signal(
            barrier, inc=1, device_id={"seq": peer // (2 * T), "tile": peer // 2 % T, "chan": peer % 2},
            device_id_type=MESH,
        )
    pl.semaphore_wait(barrier, size - 1)

    def remote(src, dst, send, recv_, **where):
        return pltpu.make_async_remote_copy(
            src_ref=src, dst_ref=dst, send_sem=send, recv_sem=recv_, device_id=where, device_id_type=MESH
        )

    def main_copy(k):
        d = (s + S - k) % S
        return remote(main_ref.at[pl.ds(d * COLS_DEV, wide)], recv.at[c, s], a_send.at[k], a_recv.at[k],
                      seq=d, tile=t, chan=c)

    def main_arrival(k):
        q = (s + k) % S
        return remote(main_ref.at[pl.ds(0, wide)], recv.at[c, q], a_send.at[k], a_recv.at[k], seq=q, tile=t, chan=c)

    own_copy = pltpu.make_async_copy(main_ref.at[pl.ds(s * COLS_DEV, wide)], recv.at[c, s], a_recv.at[0])

    def pass_on(k):
        q = (s + k) % S
        return remote(recv.at[c, q], recv.at[c, q], f_send.at[k], f_recv.at[k], seq=s, tile=t, chan=other)

    def passed(k):
        q = (s + k) % S
        return remote(recv.at[other, q], recv.at[other, q], f_send.at[k], f_recv.at[k], seq=s, tile=t, chan=other)

    def halo_copy(side, k):
        d = (s + S - k) % S
        src = tops_ref if side == 0 else bots_ref
        to = t + 1 if side == 0 else t - 1
        return remote(src.at[d], halo.at[c, side, s], h_send.at[side, k], h_recv.at[side, k], seq=d, tile=to, chan=c)

    def halo_arrival(side, k):
        q = (s + k) % S
        return remote(tops_ref.at[0], halo.at[c, side, q], h_send.at[side, k], h_recv.at[side, k],
                      seq=q, tile=t, chan=other)

    def halo_on(side, k):
        q = (s + k) % S
        return remote(halo.at[c, side, q], halo.at[c, side, q], g_send.at[side, k], g_recv.at[side, k],
                      seq=s, tile=t, chan=other)

    def halo_passed(side, k):
        q = (s + k) % S
        return remote(halo.at[other, side, q], halo.at[other, side, q], g_send.at[side, k], g_recv.at[side, k],
                      seq=s, tile=t, chan=other)

    sends_halo = (t < T - 1, t > 0)
    gets_halo = (t > 0, t < T - 1)

    own_copy.start()
    for k in range(S - 1, 0, -1):
        main_copy(k).start()
    for side in range(2):
        @pl.when(sends_halo[side])
        def _():
            for k in range(S):
                halo_copy(side, k).start()

        @pl.when(jnp.logical_not(gets_halo[side]))
        def _():
            halo[:, side] = jnp.zeros(halo.shape[:1] + halo.shape[2:], halo.dtype)

    @pl.when(s == 0)
    def _():
        mid[:, 0] = jnp.zeros(mid.shape[:1] + mid.shape[2:], mid.dtype)

    @pl.when(s == S - 1)
    def _():
        mid[:, wide - 1] = jnp.zeros(mid.shape[:1] + mid.shape[2:], mid.dtype)

    act3[:, 0:2] = jnp.zeros((wide, 2) + act3.shape[2:], act3.dtype)

    out_half = uw_ref.shape[3]
    source = lax.broadcasted_iota(jnp.int32, (out_half, 2 * out_half), 0)
    target = lax.broadcasted_iota(jnp.int32, (out_half, 2 * out_half), 1)
    spread = [jnp.where(target == 2 * source + j, 1.0, 0.0).astype(jnp.bfloat16) for j in range(2)]
    row_taps = (((0,), (1, 2)), ((0, 1), (2,)))
    col_taps = (((0,), ()), ((1, 2), (0, 1)), ((), (2,)))
    for i in range(2):
        for b in range(3):
            for a in range(2):
                total = None
                for j in range(2):
                    if not col_taps[b][j]:
                        continue
                    terms = [uw_ref[dr, dc].astype(jnp.float32) for dr in row_taps[i][a] for dc in col_taps[b][j]]
                    value = functools.reduce(lambda u, v: u + v, terms).astype(jnp.bfloat16)
                    part = jnp.dot(value, spread[j], preferred_element_type=jnp.float32)
                    total = part if total is None else total + part
                wf[i, b, a * full:(a + 1) * full] = total.astype(jnp.bfloat16)

    gain = gain_ref[...]

    @pl.loop(0, S)
    def _(k):
        q = (s + k) % S

        @pl.when(k == 0)
        def _():
            own_copy.wait()

        @pl.when(k > 0)
        def _():
            main_arrival(k).wait_recv()

        pass_on(k).start()
        for side in range(2):
            @pl.when(gets_halo[side])
            def _():
                halo_arrival(side, k).wait_recv()
                halo_on(side, k).start()

        passed(k).wait_recv()
        for side in range(2):
            @pl.when(gets_halo[side])
            def _():
                halo_passed(side, k).wait_recv()

        def both(ref_of):
            return jnp.concatenate([ref_of(0).astype(jnp.float32), ref_of(1).astype(jnp.float32)], axis=-1)

        edges = [both(lambda h: halo[h, side, q]) for side in range(2)]
        for x in range(wide):
            cells = both(lambda h: recv[h, q, x])
            for f in range(nf):
                at = (x * nf + f) * 2
                ext = jnp.concatenate(
                    [edges[0][at:at + 2], cells[f * ROWS_DEV:(f + 1) * ROWS_DEV], edges[1][at:at + 2],
                     jnp.zeros((PITCH - ROWS_DEV - 4, full), jnp.float32)], axis=0)
                scale = lax.rsqrt(jnp.mean(ext * ext, axis=-1, keepdims=True) + norm_eps)
                v = ext * scale * gain
                v = v / (1.0 + jnp.exp(-v))
                slot = q * nf + f
                for dh in range(3):
                    moved = v if dh == 0 else pltpu.roll(v, PITCH - dh, 0)
                    act3[x, slot + 2, :, dh * full:(dh + 1) * full] = moved.astype(jnp.bfloat16)
                if 0 < x < wide - 1:
                    moved = pltpu.roll(ext, PITCH - 1, 0)
                    own = jnp.where(c == 0, moved[:, :half], moved[:, half:])
                    res[x - 1, slot] = own.astype(jnp.bfloat16)

    for tap in taps:
        weight_copy(*tap).wait()

    def mid_copy(x):
        return remote(mid.at[c, x + 1], mid.at[c, x + 1], m_send.at[x], m_recv.at[x], seq=s, tile=t, chan=other)

    def mid_arrival(x):
        return remote(mid.at[other, x + 1], mid.at[other, x + 1], m_send.at[x], m_recv.at[x],
                      seq=s, tile=t, chan=other)

    def edge_copy(side, far):
        slot, landing = (1, wide - 1) if side == 0 else (wide - 2, 0)
        return remote(mid.at[c, slot], mid.at[c, landing], e_send.at[side, far], e_recv.at[side, far],
                      seq=s - 1 if side == 0 else s + 1, tile=t, chan=other if far else c)

    def edge_arrival(side, far):
        slot, landing = (1, wide - 1) if side == 0 else (wide - 2, 0)
        return remote(mid.at[c, slot], mid.at[other if far else c, landing], e_send.at[side, far],
                      e_recv.at[side, far], seq=s, tile=t, chan=other)

    sends_edge = (s > 0, s < S - 1)
    gets_edge = (s < S - 1, s > 0)

    row = lax.broadcasted_iota(jnp.int32, (FRAMES, PITCH, half), 1)
    outside = jnp.logical_or(jnp.logical_and(row == 0, t == 0),
                             jnp.logical_and(row == ROWS_DEV + 1, t == T - 1))

    @pl.loop(0, COLS_DEV)
    def _(i):
        x = (COLS_DEV - 1) * i % COLS_DEV
        acc = None
        for dt in range(3):
            for dw in range(3):
                lhs = act3[x + dw, dt:dt + FRAMES].reshape(FRAMES * PITCH, 3 * full)
                part = jnp.dot(lhs, wv[dt * 3 + dw], preferred_element_type=jnp.float32)
                acc = part if acc is None else acc + part
        value = acc.reshape(FRAMES, PITCH, half) + cb_ref[...] + res[x].astype(jnp.float32)
        mid[c, x + 1] = jnp.where(outside, 0.0, value).astype(jnp.bfloat16)
        mid_copy(x).start()
        for side, at in ((0, 0), (1, COLS_DEV - 1)):
            @pl.when(jnp.logical_and(x == at, sends_edge[side]))
            def _():
                edge_copy(side, 0).start()
                edge_copy(side, 1).start()

    for x in range(COLS_DEV):
        mid_arrival(x).wait_recv()
    for side in range(2):
        @pl.when(gets_edge[side])
        def _():
            edge_arrival(side, 0).wait_recv()
            edge_arrival(side, 1).wait_recv()

    @pl.loop(0, wide)
    def _(x):
        for f in range(FRAMES):
            v = jnp.concatenate([mid[0, x, f].astype(jnp.float32), mid[1, x, f].astype(jnp.float32)], axis=-1)
            for shift in range(3):
                moved = v if shift == 0 else pltpu.roll(v, PITCH - shift, 0)
                up[x, f, :, shift * full:(shift + 1) * full] = moved.astype(jnp.bfloat16)

    @pl.loop(0, COLS_DEV)
    def _(x):
        for i in range(2):
            acc = None
            for b in range(3):
                lhs = up[x + b, :, :, i * full:(i + 2) * full].reshape(FRAMES * PITCH, 2 * full)
                part = jnp.dot(lhs, wf[i, b], preferred_element_type=jnp.float32)
                acc = part if acc is None else acc + part
            value = (acc + ub_ref[...]).reshape(FRAMES, PITCH, 2 * out_half)
            out_ref[x, i] = value[:, :ROWS_DEV].astype(jnp.bfloat16)

    for k in range(S):
        if k:
            main_copy(k).wait_send()
        pass_on(k).wait_send()
    for side in range(2):
        @pl.when(sends_halo[side])
        def _():
            for k in range(S):
                halo_copy(side, k).wait_send()

        @pl.when(gets_halo[side])
        def _():
            for k in range(S):
                halo_on(side, k).wait_send()

        @pl.when(sends_edge[side])
        def _():
            edge_copy(side, 0).wait_send()
            edge_copy(side, 1).wait_send()
    for x in range(COLS_DEV):
        mid_copy(x).wait_send()


def fused_body(S, T, latents, norm_gain, conv_weight, conv_bias, upsample_weight, upsample_bias):
    half = latents.shape[2]
    full = 2 * half
    nf = FRAMES // S
    wide = COLS_DEV + 2
    width = S * COLS_DEV
    out_half = upsample_bias.shape[0]
    cells = latents[0].reshape(nf, ROWS_DEV, width, half)
    columns = jnp.pad(jnp.transpose(cells, (2, 0, 1, 3)), ((1, 1), (0, 0), (0, 0), (0, 0)))
    edge_rows = -(-wide * nf * 2 // 16) * 16

    def edges(rows):
        parts = jnp.stack([rows[d * COLS_DEV:d * COLS_DEV + wide] for d in range(S)])
        parts = parts.reshape(S, wide * nf * 2, half)
        return jnp.pad(parts, ((0, 0), (0, edge_rows - wide * nf * 2), (0, 0)))

    tops = edges(columns[:, :, ROWS_DEV - 2:])
    bots = edges(columns[:, :, :2])
    main = columns.reshape(width + 2, nf * ROWS_DEV, half)
    vmem = pl.BlockSpec(memory_space=pltpu.VMEM)
    dma = pltpu.SemaphoreType.DMA
    bf16 = jnp.bfloat16
    out = pl.pallas_call(
        functools.partial(kernel, S, T),
        out_shape=jax.ShapeDtypeStruct((COLS_DEV, 2, FRAMES, ROWS_DEV, 2 * out_half), bf16),
        in_specs=[vmem, vmem, vmem, vmem, pl.BlockSpec(memory_space=pl.ANY), vmem, vmem, vmem],
        out_specs=vmem,
        scratch_shapes=[
            pltpu.VMEM((2, S, wide, nf * ROWS_DEV, half), bf16),
            pltpu.VMEM((2, 2, S, edge_rows, half), bf16),
            pltpu.VMEM((wide, FRAMES + 2, PITCH, 3 * full), bf16),
            pltpu.VMEM((COLS_DEV, FRAMES, PITCH, half), bf16),
            pltpu.VMEM((9, 3 * full, half), bf16),
            pltpu.VMEM((2, 3, 2 * full, 2 * out_half), bf16),
            pltpu.VMEM((2, wide, FRAMES, PITCH, half), bf16),
            pltpu.VMEM((wide, FRAMES, PITCH, 3 * full), bf16),
            dma((3, 3, 3)), dma((S,)), dma((S,)), dma((S,)), dma((S,)),
            dma((2, S)), dma((2, S)), dma((2, S)), dma((2, S)),
            dma((COLS_DEV,)), dma((COLS_DEV,)), dma((2, 2)), dma((2, 2)),
        ],
        compiler_params=pltpu.CompilerParams(
            collective_id=0, has_side_effects=True, vmem_limit_bytes=48 * 1024 * 1024
        ),
    )(main, tops, bots, norm_gain.reshape(1, full), conv_weight, conv_bias.reshape(1, half),
      upsample_weight, jnp.repeat(upsample_bias, 2).reshape(1, 2 * out_half))
    return jnp.transpose(out, (2, 3, 1, 0, 4)).reshape(FRAMES, 2 * ROWS_DEV, COLS_DEV, 2 * out_half)


def solution(mesh):
    S, T = mesh.shape["seq"], mesh.shape["tile"]
    if FRAMES % S == 0 and mesh.shape["chan"] == 2:
        body = functools.partial(fused_body, S, T)
    else:
        body = plain_body
    in_specs = (
        P("tile", ("groups", "seq"), "chan"),
        P(),
        P(None, None, None, None, "chan"),
        P("chan"),
        P(None, None, None, "chan"),
        P("chan"),
    )
    out_specs = P(None, ("groups", "tile"), "seq", "chan")
    return jax.shard_map(body, mesh=mesh, in_specs=in_specs, out_specs=out_specs, check_vma=False)
```

```python
import functools

import jax
import jax.numpy as jnp
from jax import lax
from jax.experimental import pallas as pl
from jax.experimental.pallas import tpu as pltpu
from jax.sharding import PartitionSpec as P

FRAMES = 8
ROWS_DEV = 24
COLS_DEV = 5
PITCH = 32
MESH = pl.DeviceIdType.MESH


norm_eps = 1e-06


def extended(cells, sides, width):
    for axis, dim in sides:
        count = lax.axis_size(axis)
        ends = count - 1
        head = lax.slice_in_dim(cells, 0, width, axis=dim)
        tail = lax.slice_in_dim(cells, cells.shape[dim] - width, cells.shape[dim], axis=dim)
        cells = jnp.concatenate(
            [
                lax.ppermute(tail, axis, [(i, (i + 1) % count) for i in range(ends)]),
                cells,
                lax.ppermute(head, axis, [((i + 1) % count, i) for i in range(ends)]),
            ],
            axis=dim,
        )
    return cells


def activate(padded, norm_gain):
    values = padded.astype(jnp.float32)
    scale = lax.rsqrt(jnp.mean(values * values, axis=-1, keepdims=True) + norm_eps)
    return jax.nn.silu(values * scale * norm_gain).astype(jnp.bfloat16)


def plain_body(latents, norm_gain, conv_weight, conv_bias, upsample_weight, upsample_bias):
    seq_count = lax.axis_size("seq")
    local_chan = conv_bias.shape[0]
    rows_src = FRAMES * ROWS_DEV // seq_count
    whole = lax.all_gather(latents[0], "chan", axis=1, tiled=True)
    arranged = whole.reshape(rows_src, seq_count, COLS_DEV, whole.shape[1])
    regrouped = lax.all_to_all(arranged, "seq", split_axis=1, concat_axis=0, tiled=True)
    full_field = regrouped.reshape(FRAMES, ROWS_DEV, COLS_DEV, whole.shape[1])
    padded = extended(full_field, (("seq", 2), ("tile", 1)), 1)
    field_own = lax.dynamic_slice_in_dim(
        full_field, lax.axis_index("chan") * local_chan, local_chan, 3
    )
    activation = activate(padded, norm_gain)
    shifted = jnp.pad(activation, ((2, 0), (0, 0), (0, 0), (0, 0)))
    conv_out = lax.conv_general_dilated(
        shifted[None],
        conv_weight,
        (1, 1, 1),
        "VALID",
        dimension_numbers=("NDHWC", "DHWIO", "NDHWC"),
        preferred_element_type=jnp.float32,
    )[0]
    middle = (field_own.astype(jnp.float32) + conv_out + conv_bias).astype(jnp.bfloat16)
    middle_rim = extended(middle, (("seq", 2), ("tile", 1)), 1)
    middle_full = lax.all_gather(middle_rim, "chan", axis=3, tiled=True)
    upsampled = jnp.repeat(jnp.repeat(middle_full, 2, axis=1), 2, axis=2)[:, 1:-1, 1:-1, :]
    image = lax.conv_general_dilated(
        upsampled,
        upsample_weight,
        (1, 1),
        "VALID",
        dimension_numbers=("NHWC", "HWIO", "NHWC"),
        preferred_element_type=jnp.float32,
    )
    image = image + upsample_bias
    out_chan = upsample_bias.shape[0]
    image = image.reshape(FRAMES, 2 * ROWS_DEV, COLS_DEV, 2, out_chan)
    image = jnp.transpose(image, (0, 1, 2, 4, 3)).reshape(
        FRAMES, 2 * ROWS_DEV, COLS_DEV, 2 * out_chan
    )
    return image.astype(jnp.bfloat16)


def kernel(S, T, main_ref, tops_ref, bots_ref, gain_ref, cw_ref, cb_ref, uw_ref, ub_ref, out_ref,
           recv, halo, act3, total_ref, res, wv, wf, mid, up,
           w_sem, a_send, a_recv, f_send, f_recv, h_send, h_recv, g_send, g_recv, m_send, m_recv, e_send, e_recv):
    s, t, c = lax.axis_index("seq"), lax.axis_index("tile"), lax.axis_index("chan")
    other = 1 - c
    wide = COLS_DEV + 2
    nf = FRAMES // S
    half = cb_ref.shape[1]
    full = 2 * half

    def weight_copy(dt, dh, dw):
        return pltpu.make_async_copy(
            cw_ref.at[dt, dh, dw],
            wv.at[dt * 3 + dw, :, pl.ds(dh * full, full)],
            w_sem.at[dt, dh, dw],
        )

    taps = [(dt, dh, dw) for dt in range(3) for dh in range(3) for dw in range(3)]
    for tap in taps:
        weight_copy(*tap).start()

    barrier = pltpu.get_barrier_semaphore()
    size = S * T * 2
    me = (s * T + t) * 2 + c
    for k in range(1, size):
        peer = (me + k) % size
        pl.semaphore_signal(
            barrier, inc=1, device_id={"seq": peer // (2 * T), "tile": peer // 2 % T, "chan": peer % 2},
            device_id_type=MESH,
        )
    pl.semaphore_wait(barrier, size - 1)

    def remote(src, dst, send, recv_, **where):
        return pltpu.make_async_remote_copy(
            src_ref=src, dst_ref=dst, send_sem=send, recv_sem=recv_, device_id=where, device_id_type=MESH
        )

    def main_copy(k):
        d = (s + S - k) % S
        return remote(main_ref.at[pl.ds(d * COLS_DEV, wide)], recv.at[c, s], a_send.at[k], a_recv.at[k],
                      seq=d, tile=t, chan=c)

    def main_arrival(k):
        q = (s + k) % S
        return remote(main_ref.at[pl.ds(0, wide)], recv.at[c, q], a_send.at[k], a_recv.at[k], seq=q, tile=t, chan=c)

    own_copy = pltpu.make_async_copy(main_ref.at[pl.ds(s * COLS_DEV, wide)], recv.at[c, s], a_recv.at[0])

    def pass_on(k):
        q = (s + k) % S
        return remote(recv.at[c, q], recv.at[c, q], f_send.at[k], f_recv.at[k], seq=s, tile=t, chan=other)

    def passed(k):
        q = (s + k) % S
        return remote(recv.at[other, q], recv.at[other, q], f_send.at[k], f_recv.at[k], seq=s, tile=t, chan=other)

    def halo_copy(side, k):
        d = (s + S - k) % S
        src = tops_ref if side == 0 else bots_ref
        to = t + 1 if side == 0 else t - 1
        return remote(src.at[d], halo.at[c, side, s], h_send.at[side, k], h_recv.at[side, k], seq=d, tile=to, chan=c)

    def halo_arrival(side, k):
        q = (s + k) % S
        return remote(tops_ref.at[0], halo.at[c, side, q], h_send.at[side, k], h_recv.at[side, k],
                      seq=q, tile=t, chan=other)

    def halo_on(side, k):
        q = (s + k) % S
        return remote(halo.at[c, side, q], halo.at[c, side, q], g_send.at[side, k], g_recv.at[side, k],
                      seq=s, tile=t, chan=other)

    def halo_passed(side, k):
        q = (s + k) % S
        return remote(halo.at[other, side, q], halo.at[other, side, q], g_send.at[side, k], g_recv.at[side, k],
                      seq=s, tile=t, chan=other)

    sends_halo = (t < T - 1, t > 0)
    gets_halo = (t > 0, t < T - 1)

    own_copy.start()
    for k in range(S - 1, 0, -1):
        main_copy(k).start()
    for side in range(2):
        @pl.when(sends_halo[side])
        def _():
            for k in range(S):
                halo_copy(side, k).start()

        @pl.when(jnp.logical_not(gets_halo[side]))
        def _():
            halo[:, side] = jnp.zeros(halo.shape[:1] + halo.shape[2:], halo.dtype)

    @pl.when(s == 0)
    def _():
        mid[:, 0] = jnp.zeros(mid.shape[:1] + mid.shape[2:], mid.dtype)

    @pl.when(s == S - 1)
    def _():
        mid[:, wide - 1] = jnp.zeros(mid.shape[:1] + mid.shape[2:], mid.dtype)

    total_ref[...] = jnp.zeros(total_ref.shape, total_ref.dtype)

    out_half = uw_ref.shape[2]
    source = lax.broadcasted_iota(jnp.int32, (2 * out_half, out_half), 1)
    target = lax.broadcasted_iota(jnp.int32, (2 * out_half, out_half), 0)
    spread = [jnp.where(target == 2 * source + j, 1.0, 0.0).astype(jnp.bfloat16) for j in range(2)]
    row_taps = (((0,), (1, 2)), ((0, 1), (2,)))
    col_taps = (((0,), ()), ((1, 2), (0, 1)), ((), (2,)))
    for i in range(2):
        for b in range(3):
            for a in range(2):
                total = None
                for j in range(2):
                    if not col_taps[b][j]:
                        continue
                    terms = [uw_ref[dr, dc].astype(jnp.float32) for dr in row_taps[i][a] for dc in col_taps[b][j]]
                    value = functools.reduce(lambda u, v: u + v, terms).astype(jnp.bfloat16)
                    part = jnp.dot(spread[j], value, preferred_element_type=jnp.float32)
                    total = part if total is None else total + part
                wf[i, b, :, a * full:(a + 1) * full] = total.astype(jnp.bfloat16)

    gain = gain_ref[...]

    def dot(lhs, rhs):
        return lax.dot_general(lhs, rhs, (((1,), (1,)), ((), ())), preferred_element_type=jnp.float32)

    for tap in taps:
        weight_copy(*tap).wait()

    @pl.loop(0, S)
    def _(k):
        q = (s + k) % S

        @pl.when(k == 0)
        def _():
            own_copy.wait()

        @pl.when(k > 0)
        def _():
            main_arrival(k).wait_recv()

        pass_on(k).start()
        for side in range(2):
            @pl.when(gets_halo[side])
            def _():
                halo_arrival(side, k).wait_recv()
                halo_on(side, k).start()

        passed(k).wait_recv()
        for side in range(2):
            @pl.when(gets_halo[side])
            def _():
                halo_passed(side, k).wait_recv()

        def both(ref_of):
            parts = [ref_of(h).astype(jnp.float32) for h in range(2)]
            return [jnp.concatenate([p[:, f * half:(f + 1) * half] for p in parts], axis=-1) for f in range(nf)]

        edges = [both(lambda h: halo[h, side, q]) for side in range(2)]
        for x in range(wide):
            cells = both(lambda h: recv[h, q, x])
            for f in range(nf):
                at = x * 2
                ext = jnp.concatenate(
                    [edges[0][f][at:at + 2], cells[f], edges[1][f][at:at + 2],
                     jnp.zeros((PITCH - ROWS_DEV - 4, full), jnp.float32)], axis=0)
                scale = lax.rsqrt(jnp.mean(ext * ext, axis=-1, keepdims=True) + norm_eps)
                v = ext * scale * gain
                v = v / (1.0 + jnp.exp(-v))
                slot = q * nf + f
                for dh in range(3):
                    moved = v if dh == 0 else pltpu.roll(v, PITCH - dh, 0)
                    act3[x, f, :, dh * full:(dh + 1) * full] = moved.astype(jnp.bfloat16)
                if 0 < x < wide - 1:
                    moved = pltpu.roll(ext, PITCH - 1, 0)
                    own = jnp.where(c == 0, moved[:, :half], moved[:, half:])
                    res[x - 1, slot] = own.astype(jnp.bfloat16)

        for dt in range(3):
            acc = None
            for dw in range(3):
                lhs = act3[dw:dw + COLS_DEV].reshape(COLS_DEV * nf * PITCH, 3 * full)
                part = dot(lhs, wv[dt * 3 + dw])
                acc = part if acc is None else acc + part
            total_ref[:, pl.ds(q * nf + 2 - dt, nf)] += acc.reshape(COLS_DEV, nf, PITCH, half)

    def mid_copy(x):
        return remote(mid.at[c, x + 1], mid.at[c, x + 1], m_send.at[x], m_recv.at[x], seq=s, tile=t, chan=other)

    def mid_arrival(x):
        return remote(mid.at[other, x + 1], mid.at[other, x + 1], m_send.at[x], m_recv.at[x],
                      seq=s, tile=t, chan=other)

    def edge_copy(side):
        slot, landing = (1, wide - 1) if side == 0 else (wide - 2, 0)
        return remote(mid.at[c, slot], mid.at[c, landing], e_send.at[side, 0], e_recv.at[side, 0],
                      seq=s - 1 if side == 0 else s + 1, tile=t, chan=c)

    def edge_on(side):
        landing = wide - 1 if side == 0 else 0
        return remote(mid.at[c, landing], mid.at[c, landing], e_send.at[side, 1], e_recv.at[side, 1],
                      seq=s, tile=t, chan=other)

    def edge_passed(side):
        landing = wide - 1 if side == 0 else 0
        return remote(mid.at[other, landing], mid.at[other, landing], e_send.at[side, 1], e_recv.at[side, 1],
                      seq=s, tile=t, chan=other)

    sends_edge = (s > 0, s < S - 1)
    gets_edge = (s < S - 1, s > 0)

    row = lax.broadcasted_iota(jnp.int32, (FRAMES, PITCH, half), 1)
    outside = jnp.logical_or(jnp.logical_and(row == 0, t == 0),
                             jnp.logical_and(row == ROWS_DEV + 1, t == T - 1))

    @pl.loop(0, COLS_DEV)
    def _(i):
        x = (COLS_DEV - 1) * i % COLS_DEV
        value = total_ref[x, 0:FRAMES] + cb_ref[...] + res[x].astype(jnp.float32)
        mid[c, x + 1] = jnp.where(outside, 0.0, value).astype(jnp.bfloat16)
        for side, at in ((0, 0), (1, COLS_DEV - 1)):
            @pl.when(jnp.logical_and(x == at, sends_edge[side]))
            def _():
                edge_copy(side).start()
        mid_copy(x).start()

    for x in range(COLS_DEV):
        mid_arrival(x).wait_recv()

    def lay(x):
        for f in range(FRAMES):
            v = jnp.concatenate([mid[0, x, f].astype(jnp.float32), mid[1, x, f].astype(jnp.float32)], axis=-1)
            for shift in range(3):
                moved = v if shift == 0 else pltpu.roll(v, PITCH - shift, 0)
                up[x, f, :, shift * full:(shift + 1) * full] = moved.astype(jnp.bfloat16)

    def emit(x):
        for i in range(2):
            acc = None
            for b in range(3):
                lhs = up[x + b, :, :, i * full:(i + 2) * full].reshape(FRAMES * PITCH, 2 * full)
                part = dot(lhs, wf[i, b])
                acc = part if acc is None else acc + part
            value = (acc + ub_ref[...]).reshape(FRAMES, PITCH, 2 * out_half)
            out_ref[x, i] = value[:, :ROWS_DEV].astype(jnp.bfloat16)

    @pl.loop(1, wide - 1)
    def _(x):
        lay(x)

    for side in range(2):
        @pl.when(gets_edge[side])
        def _():
            edge_copy(side).wait_recv()
            edge_on(side).start()

    @pl.loop(1, COLS_DEV - 1)
    def _(x):
        emit(x)

    for side in range(2):
        @pl.when(gets_edge[side])
        def _():
            edge_passed(side).wait_recv()

    @pl.loop(0, 2)
    def _(i):
        lay(i * (wide - 1))

    @pl.loop(0, 2)
    def _(i):
        emit(i * (COLS_DEV - 1))

    for k in range(S):
        if k:
            main_copy(k).wait_send()
        pass_on(k).wait_send()
    for side in range(2):
        @pl.when(sends_halo[side])
        def _():
            for k in range(S):
                halo_copy(side, k).wait_send()

        @pl.when(gets_halo[side])
        def _():
            for k in range(S):
                halo_on(side, k).wait_send()

        @pl.when(sends_edge[side])
        def _():
            edge_copy(side).wait_send()

        @pl.when(gets_edge[side])
        def _():
            edge_on(side).wait_send()
    for x in range(COLS_DEV):
        mid_copy(x).wait_send()


def fused_body(S, T, latents, norm_gain, conv_weight, conv_bias, upsample_weight, upsample_bias):
    half = latents.shape[2]
    full = 2 * half
    nf = FRAMES // S
    wide = COLS_DEV + 2
    width = S * COLS_DEV
    out_half = upsample_bias.shape[0]
    cells = latents[0].reshape(nf, ROWS_DEV, width, half)
    main = jnp.transpose(cells, (2, 1, 0, 3)).reshape(width, ROWS_DEV, nf * half)
    main = jnp.pad(main, ((1, 1), (0, 0), (0, 0)))
    edge_rows = -(-wide * 2 // 16) * 16

    def edges(rows):
        parts = jnp.stack([rows[d * COLS_DEV:d * COLS_DEV + wide] for d in range(S)])
        parts = parts.reshape(S, wide * 2, nf * half)
        return jnp.pad(parts, ((0, 0), (0, edge_rows - wide * 2), (0, 0)))

    tops = edges(main[:, ROWS_DEV - 2:])
    bots = edges(main[:, :2])
    vmem = pl.BlockSpec(memory_space=pltpu.VMEM)
    dma = pltpu.SemaphoreType.DMA
    bf16 = jnp.bfloat16
    out = pl.pallas_call(
        functools.partial(kernel, S, T),
        out_shape=jax.ShapeDtypeStruct((COLS_DEV, 2, FRAMES, ROWS_DEV, 2 * out_half), bf16),
        in_specs=[vmem, vmem, vmem, vmem, pl.BlockSpec(memory_space=pltpu.HBM), vmem, vmem, vmem],
        out_specs=vmem,
        scratch_shapes=[
            pltpu.VMEM((2, S, wide, ROWS_DEV, nf * half), bf16),
            pltpu.VMEM((2, 2, S, edge_rows, nf * half), bf16),
            pltpu.VMEM((wide, nf, PITCH, 3 * full), bf16),
            pltpu.VMEM((COLS_DEV, FRAMES + 2, PITCH, half), jnp.float32),
            pltpu.VMEM((COLS_DEV, FRAMES, PITCH, half), bf16),
            pltpu.VMEM((9, half, 3 * full), bf16),
            pltpu.VMEM((2, 3, 2 * out_half, 2 * full), bf16),
            pltpu.VMEM((2, wide, FRAMES, PITCH, half), bf16),
            pltpu.VMEM((wide, FRAMES, PITCH, 3 * full), bf16),
            dma((3, 3, 3)), dma((S,)), dma((S,)), dma((S,)), dma((S,)),
            dma((2, S)), dma((2, S)), dma((2, S)), dma((2, S)),
            dma((COLS_DEV,)), dma((COLS_DEV,)), dma((2, 2)), dma((2, 2)),
        ],
        compiler_params=pltpu.CompilerParams(
            collective_id=0, has_side_effects=True, vmem_limit_bytes=48 * 1024 * 1024
        ),
    )(main, tops, bots, norm_gain.reshape(1, full), jnp.transpose(conv_weight, (0, 1, 2, 4, 3)),
      conv_bias.reshape(1, half), jnp.transpose(upsample_weight, (0, 1, 3, 2)), jnp.repeat(upsample_bias, 2).reshape(1, 2 * out_half))
    return jnp.transpose(out, (2, 3, 1, 0, 4)).reshape(FRAMES, 2 * ROWS_DEV, COLS_DEV, 2 * out_half)


def solution(mesh):
    S, T = mesh.shape["seq"], mesh.shape["tile"]
    if FRAMES % S == 0 and mesh.shape["chan"] == 2:
        body = functools.partial(fused_body, S, T)
    else:
        body = plain_body
    in_specs = (
        P("tile", ("groups", "seq"), "chan"),
        P(),
        P(None, None, None, None, "chan"),
        P("chan"),
        P(None, None, None, "chan"),
        P("chan"),
    )
    out_specs = P(None, ("groups", "tile"), "seq", "chan")
    return jax.shard_map(body, mesh=mesh, in_specs=in_specs, out_specs=out_specs, check_vma=False)
```

```python
import functools

import jax
import jax.numpy as jnp
from jax import lax
from jax.experimental import pallas as pl
from jax.experimental.pallas import tpu as pltpu
from jax.sharding import PartitionSpec as P

FRAMES = 8
ROWS_DEV = 24
COLS_DEV = 5
PITCH = 32
MESH = pl.DeviceIdType.MESH


norm_eps = 1e-06


def extended(cells, sides, width):
    for axis, dim in sides:
        count = lax.axis_size(axis)
        ends = count - 1
        head = lax.slice_in_dim(cells, 0, width, axis=dim)
        tail = lax.slice_in_dim(cells, cells.shape[dim] - width, cells.shape[dim], axis=dim)
        cells = jnp.concatenate(
            [
                lax.ppermute(tail, axis, [(i, (i + 1) % count) for i in range(ends)]),
                cells,
                lax.ppermute(head, axis, [((i + 1) % count, i) for i in range(ends)]),
            ],
            axis=dim,
        )
    return cells


def activate(padded, norm_gain):
    values = padded.astype(jnp.float32)
    scale = lax.rsqrt(jnp.mean(values * values, axis=-1, keepdims=True) + norm_eps)
    return jax.nn.silu(values * scale * norm_gain).astype(jnp.bfloat16)


def plain_body(latents, norm_gain, conv_weight, conv_bias, upsample_weight, upsample_bias):
    seq_count = lax.axis_size("seq")
    local_chan = conv_bias.shape[0]
    rows_src = FRAMES * ROWS_DEV // seq_count
    whole = lax.all_gather(latents[0], "chan", axis=1, tiled=True)
    arranged = whole.reshape(rows_src, seq_count, COLS_DEV, whole.shape[1])
    regrouped = lax.all_to_all(arranged, "seq", split_axis=1, concat_axis=0, tiled=True)
    full_field = regrouped.reshape(FRAMES, ROWS_DEV, COLS_DEV, whole.shape[1])
    padded = extended(full_field, (("seq", 2), ("tile", 1)), 1)
    field_own = lax.dynamic_slice_in_dim(
        full_field, lax.axis_index("chan") * local_chan, local_chan, 3
    )
    activation = activate(padded, norm_gain)
    shifted = jnp.pad(activation, ((2, 0), (0, 0), (0, 0), (0, 0)))
    conv_out = lax.conv_general_dilated(
        shifted[None],
        conv_weight,
        (1, 1, 1),
        "VALID",
        dimension_numbers=("NDHWC", "DHWIO", "NDHWC"),
        preferred_element_type=jnp.float32,
    )[0]
    middle = (field_own.astype(jnp.float32) + conv_out + conv_bias).astype(jnp.bfloat16)
    middle_rim = extended(middle, (("seq", 2), ("tile", 1)), 1)
    middle_full = lax.all_gather(middle_rim, "chan", axis=3, tiled=True)
    upsampled = jnp.repeat(jnp.repeat(middle_full, 2, axis=1), 2, axis=2)[:, 1:-1, 1:-1, :]
    image = lax.conv_general_dilated(
        upsampled,
        upsample_weight,
        (1, 1),
        "VALID",
        dimension_numbers=("NHWC", "HWIO", "NHWC"),
        preferred_element_type=jnp.float32,
    )
    image = image + upsample_bias
    out_chan = upsample_bias.shape[0]
    image = image.reshape(FRAMES, 2 * ROWS_DEV, COLS_DEV, 2, out_chan)
    image = jnp.transpose(image, (0, 1, 2, 4, 3)).reshape(
        FRAMES, 2 * ROWS_DEV, COLS_DEV, 2 * out_chan
    )
    return image.astype(jnp.bfloat16)


def kernel(S, T, main_ref, tops_ref, bots_ref, gain_ref, cw_ref, cb_ref, uw_ref, ub_ref, out_ref,
           recv, halo, act3, total_ref, res, wv, wf, mid, up, image_bias,
           w_sem, a_send, a_recv, f_send, f_recv, h_send, h_recv, g_send, g_recv, m_send, m_recv, e_send, e_recv):
    s, t, c = lax.axis_index("seq"), lax.axis_index("tile"), lax.axis_index("chan")
    other = 1 - c
    wide = COLS_DEV + 2
    nf = FRAMES // S
    half = cb_ref.shape[1]
    full = 2 * half

    def weight_copy(dt, dh, dw):
        return pltpu.make_async_copy(
            cw_ref.at[dt, dh, dw],
            wv.at[dt * 3 + dw, :, pl.ds(dh * full, full)],
            w_sem.at[dt, dh, dw],
        )

    taps = [(dt, dh, dw) for dt in range(3) for dh in range(3) for dw in range(3)]
    for tap in taps:
        weight_copy(*tap).start()

    barrier = pltpu.get_barrier_semaphore()
    size = S * T * 2
    me = (s * T + t) * 2 + c
    for k in range(1, size):
        peer = (me + k) % size
        pl.semaphore_signal(
            barrier, inc=1, device_id={"seq": peer // (2 * T), "tile": peer // 2 % T, "chan": peer % 2},
            device_id_type=MESH,
        )
    pl.semaphore_wait(barrier, size - 1)

    def remote(src, dst, send, recv_, **where):
        return pltpu.make_async_remote_copy(
            src_ref=src, dst_ref=dst, send_sem=send, recv_sem=recv_, device_id=where, device_id_type=MESH
        )

    def partner(k):
        bits = [b for b in range(S.bit_length() - 1)]
        return sum(((s // 2**b + k // 2**b) % 2 * 2**b for b in bits), 0 * s)

    def main_copy(k):
        d = partner(k)
        return remote(main_ref.at[pl.ds(d * COLS_DEV, wide)], recv.at[c, s], a_send.at[k], a_recv.at[k],
                      seq=d, tile=t, chan=c)

    def main_arrival(k):
        q = partner(k)
        return remote(main_ref.at[pl.ds(0, wide)], recv.at[c, q], a_send.at[k], a_recv.at[k], seq=q, tile=t, chan=c)

    own_copy = pltpu.make_async_copy(main_ref.at[pl.ds(s * COLS_DEV, wide)], recv.at[c, s], a_recv.at[0])

    def pass_on(k):
        q = partner(k)
        return remote(recv.at[c, q], recv.at[c, q], f_send.at[k], f_recv.at[k], seq=s, tile=t, chan=other)

    def passed(k):
        q = partner(k)
        return remote(recv.at[other, q], recv.at[other, q], f_send.at[k], f_recv.at[k], seq=s, tile=t, chan=other)

    def halo_copy(side, k):
        d = partner(k)
        src = tops_ref if side == 0 else bots_ref
        to = t + 1 if side == 0 else t - 1
        return remote(src.at[d], halo.at[c, side, s], h_send.at[side, k], h_recv.at[side, k], seq=d, tile=to, chan=c)

    def halo_arrival(side, k):
        q = partner(k)
        return remote(tops_ref.at[0], halo.at[c, side, q], h_send.at[side, k], h_recv.at[side, k],
                      seq=q, tile=t, chan=other)

    def halo_on(side, k):
        q = partner(k)
        return remote(halo.at[c, side, q], halo.at[c, side, q], g_send.at[side, k], g_recv.at[side, k],
                      seq=s, tile=t, chan=other)

    def halo_passed(side, k):
        q = partner(k)
        return remote(halo.at[other, side, q], halo.at[other, side, q], g_send.at[side, k], g_recv.at[side, k],
                      seq=s, tile=t, chan=other)

    sends_halo = (t < T - 1, t > 0)
    gets_halo = (t > 0, t < T - 1)

    own_copy.start()
    for k in range(1, S):
        main_copy(k).start()
    for side in range(2):
        @pl.when(sends_halo[side])
        def _():
            for k in range(S):
                halo_copy(side, k).start()

        @pl.when(jnp.logical_not(gets_halo[side]))
        def _():
            halo[:, side] = jnp.zeros(halo.shape[:1] + halo.shape[2:], halo.dtype)

    @pl.when(s == 0)
    def _():
        mid[:, 0] = jnp.zeros(mid.shape[:1] + mid.shape[2:], mid.dtype)

    @pl.when(s == S - 1)
    def _():
        mid[:, wide - 1] = jnp.zeros(mid.shape[:1] + mid.shape[2:], mid.dtype)

    total_ref[...] = jnp.zeros(total_ref.shape, total_ref.dtype)

    out_half = uw_ref.shape[2]
    source = lax.broadcasted_iota(jnp.int32, (2 * out_half, out_half), 1)
    target = lax.broadcasted_iota(jnp.int32, (2 * out_half, out_half), 0)
    spread = [jnp.where(target == 2 * source + j, 1.0, 0.0).astype(jnp.bfloat16) for j in range(2)]
    row_taps = (((0,), (1, 2)), ((0, 1), (2,)))
    col_taps = (((0,), ()), ((1, 2), (0, 1)), ((), (2,)))
    for i in range(2):
        for b in range(3):
            for a in range(2):
                total = None
                for j in range(2):
                    if not col_taps[b][j]:
                        continue
                    terms = [uw_ref[dr, dc].astype(jnp.float32) for dr in row_taps[i][a] for dc in col_taps[b][j]]
                    value = functools.reduce(lambda u, v: u + v, terms).astype(jnp.bfloat16)
                    part = jnp.dot(spread[j], value, preferred_element_type=jnp.float32)
                    total = part if total is None else total + part
                wf[i, b, :, a * full:(a + 1) * full] = total.astype(jnp.bfloat16)

    both_bias = sum(
        lax.dot_general(jnp.broadcast_to(ub_ref[...], (8, out_half)), m.astype(jnp.float32), (((1,), (1,)), ((), ())),
                        precision=lax.Precision.HIGHEST, preferred_element_type=jnp.float32)
        for m in spread)
    image_bias[...] = both_bias[:1]
    gain = gain_ref[...]

    def dot(lhs, rhs):
        return lax.dot_general(lhs, rhs, (((1,), (1,)), ((), ())), preferred_element_type=jnp.float32)

    for tap in taps:
        weight_copy(*tap).wait()

    @pl.loop(0, S)
    def _(k):
        q = partner(k)

        @pl.when(k == 0)
        def _():
            own_copy.wait()

        @pl.when(k > 0)
        def _():
            main_arrival(k).wait_recv()

        pass_on(k).start()
        for side in range(2):
            @pl.when(gets_halo[side])
            def _():
                halo_arrival(side, k).wait_recv()
                halo_on(side, k).start()

        passed(k).wait_recv()
        for side in range(2):
            @pl.when(gets_halo[side])
            def _():
                halo_passed(side, k).wait_recv()

        def both(ref_of):
            parts = [ref_of(h).astype(jnp.float32) for h in range(2)]
            return [jnp.concatenate([p[:, f * half:(f + 1) * half] for p in parts], axis=-1) for f in range(nf)]

        edges = [both(lambda h: halo[h, side, q]) for side in range(2)]
        for x in range(wide):
            cells = both(lambda h: recv[h, q, x])
            for f in range(nf):
                at = x * 2
                ext = jnp.concatenate(
                    [edges[0][f][at:at + 2], cells[f], edges[1][f][at:at + 2],
                     jnp.zeros((PITCH - ROWS_DEV - 4, full), jnp.float32)], axis=0)
                scale = lax.rsqrt(jnp.mean(ext * ext, axis=-1, keepdims=True) + norm_eps)
                v = ext * scale * gain
                v = 0.5 * v * (1.0 + jnp.tanh(0.5 * v))
                slot = q * nf + f
                for dh in range(3):
                    moved = v if dh == 0 else pltpu.roll(v, PITCH - dh, 0)
                    act3[x, f, :, dh * full:(dh + 1) * full] = moved.astype(jnp.bfloat16)
                if 0 < x < wide - 1:
                    moved = pltpu.roll(ext, PITCH - 1, 0)
                    own = jnp.where(c == 0, moved[:, :half], moved[:, half:])
                    res[x - 1, slot] = own.astype(jnp.bfloat16)

        for dt in range(3):
            acc = None
            for dw in range(3):
                lhs = act3[dw:dw + COLS_DEV].reshape(COLS_DEV * nf * PITCH, 3 * full)
                part = dot(lhs, wv[dt * 3 + dw])
                acc = part if acc is None else acc + part
            total_ref[:, pl.ds(q * nf + 2 - dt, nf)] += acc.reshape(COLS_DEV, nf, PITCH, half)

    def mid_copy(x):
        return remote(mid.at[c, x + 1], mid.at[c, x + 1], m_send.at[x], m_recv.at[x], seq=s, tile=t, chan=other)

    def mid_arrival(x):
        return remote(mid.at[other, x + 1], mid.at[other, x + 1], m_send.at[x], m_recv.at[x],
                      seq=s, tile=t, chan=other)

    def edge_copy(side):
        slot, landing = (1, wide - 1) if side == 0 else (wide - 2, 0)
        return remote(mid.at[c, slot], mid.at[c, landing], e_send.at[side, 0], e_recv.at[side, 0],
                      seq=s - 1 if side == 0 else s + 1, tile=t, chan=c)

    def edge_on(side):
        landing = wide - 1 if side == 0 else 0
        return remote(mid.at[c, landing], mid.at[c, landing], e_send.at[side, 1], e_recv.at[side, 1],
                      seq=s, tile=t, chan=other)

    def edge_passed(side):
        landing = wide - 1 if side == 0 else 0
        return remote(mid.at[other, landing], mid.at[other, landing], e_send.at[side, 1], e_recv.at[side, 1],
                      seq=s, tile=t, chan=other)

    sends_edge = (s > 0, s < S - 1)
    gets_edge = (s < S - 1, s > 0)

    row = lax.broadcasted_iota(jnp.int32, (FRAMES, PITCH, half), 1)
    outside = jnp.logical_or(jnp.logical_and(row == 0, t == 0),
                             jnp.logical_and(row == ROWS_DEV + 1, t == T - 1))

    @pl.loop(0, COLS_DEV)
    def _(i):
        x = (COLS_DEV - 1) * i % COLS_DEV
        value = total_ref[x, 0:FRAMES] + cb_ref[...] + res[x].astype(jnp.float32)
        mid[c, x + 1] = jnp.where(outside, 0.0, value).astype(jnp.bfloat16)
        for side, at in ((0, 0), (1, COLS_DEV - 1)):
            @pl.when(jnp.logical_and(x == at, sends_edge[side]))
            def _():
                edge_copy(side).start()
        mid_copy(x).start()

    for x in range(COLS_DEV):
        mid_arrival(x).wait_recv()

    def lay(x):
        for f in range(FRAMES):
            v = jnp.concatenate([mid[0, x, f].astype(jnp.float32), mid[1, x, f].astype(jnp.float32)], axis=-1)
            for shift in range(3):
                moved = v if shift == 0 else pltpu.roll(v, PITCH - shift, 0)
                up[x, f, :, shift * full:(shift + 1) * full] = moved.astype(jnp.bfloat16)

    def emit(x):
        for i in range(2):
            acc = None
            for b in range(3):
                lhs = up[x + b, :, :, i * full:(i + 2) * full].reshape(FRAMES * PITCH, 2 * full)
                part = dot(lhs, wf[i, b])
                acc = part if acc is None else acc + part
            value = (acc + image_bias[...]).reshape(FRAMES, PITCH, 2 * out_half)
            out_ref[x, i] = value[:, :ROWS_DEV].astype(jnp.bfloat16)

    @pl.loop(1, wide - 1)
    def _(x):
        lay(x)

    for side in range(2):
        @pl.when(gets_edge[side])
        def _():
            edge_copy(side).wait_recv()
            edge_on(side).start()

    @pl.loop(1, COLS_DEV - 1)
    def _(x):
        emit(x)

    for side in range(2):
        @pl.when(gets_edge[side])
        def _():
            edge_passed(side).wait_recv()

    @pl.loop(0, 2)
    def _(i):
        lay(i * (wide - 1))

    @pl.loop(0, 2)
    def _(i):
        emit(i * (COLS_DEV - 1))

    for k in range(S):
        if k:
            main_copy(k).wait_send()
        pass_on(k).wait_send()
    for side in range(2):
        @pl.when(sends_halo[side])
        def _():
            for k in range(S):
                halo_copy(side, k).wait_send()

        @pl.when(gets_halo[side])
        def _():
            for k in range(S):
                halo_on(side, k).wait_send()

        @pl.when(sends_edge[side])
        def _():
            edge_copy(side).wait_send()

        @pl.when(gets_edge[side])
        def _():
            edge_on(side).wait_send()
    for x in range(COLS_DEV):
        mid_copy(x).wait_send()


def fused_body(S, T, latents, norm_gain, conv_weight, conv_bias, upsample_weight, upsample_bias):
    half = latents.shape[2]
    full = 2 * half
    nf = FRAMES // S
    wide = COLS_DEV + 2
    width = S * COLS_DEV
    out_half = upsample_bias.shape[0]
    cells = latents[0].reshape(nf, ROWS_DEV, width, half)
    main = jnp.transpose(cells, (2, 1, 0, 3)).reshape(width, ROWS_DEV, nf * half)
    main = jnp.pad(main, ((1, 1), (0, 0), (0, 0)))
    edge_rows = -(-wide * 2 // 16) * 16

    def edges(rows):
        parts = jnp.stack([rows[d * COLS_DEV:d * COLS_DEV + wide] for d in range(S)])
        parts = parts.reshape(S, wide * 2, nf * half)
        return jnp.pad(parts, ((0, 0), (0, edge_rows - wide * 2), (0, 0)))

    tops = edges(main[:, ROWS_DEV - 2:])
    bots = edges(main[:, :2])
    vmem = pl.BlockSpec(memory_space=pltpu.VMEM)
    dma = pltpu.SemaphoreType.DMA
    bf16 = jnp.bfloat16
    out = pl.pallas_call(
        functools.partial(kernel, S, T),
        out_shape=jax.ShapeDtypeStruct((COLS_DEV, 2, FRAMES, ROWS_DEV, 2 * out_half), bf16),
        in_specs=[vmem, vmem, vmem, vmem, pl.BlockSpec(memory_space=pltpu.HBM), vmem, vmem, vmem],
        out_specs=vmem,
        scratch_shapes=[
            pltpu.VMEM((2, S, wide, ROWS_DEV, nf * half), bf16),
            pltpu.VMEM((2, 2, S, edge_rows, nf * half), bf16),
            pltpu.VMEM((wide, nf, PITCH, 3 * full), bf16),
            pltpu.VMEM((COLS_DEV, FRAMES + 2, PITCH, half), jnp.float32),
            pltpu.VMEM((COLS_DEV, FRAMES, PITCH, half), bf16),
            pltpu.VMEM((9, half, 3 * full), bf16),
            pltpu.VMEM((2, 3, 2 * out_half, 2 * full), bf16),
            pltpu.VMEM((2, wide, FRAMES, PITCH, half), bf16),
            pltpu.VMEM((wide, FRAMES, PITCH, 3 * full), bf16),
            pltpu.VMEM((1, 2 * out_half), jnp.float32),
            dma((3, 3, 3)), dma((S,)), dma((S,)), dma((S,)), dma((S,)),
            dma((2, S)), dma((2, S)), dma((2, S)), dma((2, S)),
            dma((COLS_DEV,)), dma((COLS_DEV,)), dma((2, 2)), dma((2, 2)),
        ],
        compiler_params=pltpu.CompilerParams(
            collective_id=0, has_side_effects=True, vmem_limit_bytes=50 * 1024 * 1024
        ),
    )(main, tops, bots, norm_gain.reshape(1, full), jnp.transpose(conv_weight, (0, 1, 2, 4, 3)),
      conv_bias.reshape(1, half), jnp.transpose(upsample_weight, (0, 1, 3, 2)), upsample_bias.reshape(1, out_half))
    return jnp.transpose(out, (2, 3, 1, 0, 4)).reshape(FRAMES, 2 * ROWS_DEV, COLS_DEV, 2 * out_half)


def solution(mesh):
    S, T = mesh.shape["seq"], mesh.shape["tile"]
    if FRAMES % S == 0 and mesh.shape["chan"] == 2:
        body = functools.partial(fused_body, S, T)
    else:
        body = plain_body
    in_specs = (
        P("tile", ("groups", "seq"), "chan"),
        P(),
        P(None, None, None, None, "chan"),
        P("chan"),
        P(None, None, None, "chan"),
        P("chan"),
    )
    out_specs = P(None, ("groups", "tile"), "seq", "chan")
    return jax.shard_map(body, mesh=mesh, in_specs=in_specs, out_specs=out_specs, check_vma=False)
```
